512 devices in a mesh: blk: 8 (over y, core), uly: 16 (over z), tp: 4 (over x).
Axes of the slice: x: 4, y: 4, z: 16, core: 2. Of those that a mesh axis runs over, the one named last changes fastest.
Arguments:
- queries: bfloat16 [16384, 8192], P(('blk', 'uly'), 'tp'), parts along dimension 1, may hold values from -9 to 9
- keys: bfloat16 [16384, 1024], P(('blk', 'uly'), 'tp'), parts along dimension 1, may hold values from -9 to 9
- values: bfloat16 [16384, 1024], P(('blk', 'uly'), 'tp'), parts along dimension 1, may hold values from -6 to 6
- head_map: int32 [64], P('tp'), parts along dimension 0, may hold values from 0 to 1, as said below
- doc_lengths: int32 [32], replicated, may hold values from 1 to 2048, 16384 in all
- plan: int32 [8, 32], replicated, may hold values from 0 to 31, as said below
Outputs:
- output: bfloat16 [16384, 8192], P(('blk', 'uly'), 'tp'), parts along dimension 1
The draws below stay inside these ranges and needn't reach their ends.
There are 4 independent parts, one for each index of `tp`. The reference program is written for one: setup_inputs(seed, part) draws one part's arguments, and reference() takes and returns one part's arrays. A program takes and returns all parts, laid end to end along the dimension named above; an argument that names none is the same for every part. Nothing has to cross between parts.
Inputs may be any that keep to these rules, and one draw needn't show every extreme that they name: `head_map`: each key-value head serves exactly 8 query heads. Each row plan[s] is a permutation of 0 to 31.
All inputs are finite; a program needn't handle non-finite values.
Results may differ from the reference program's by a relative error of at most 0.0036.
Values may be sent and summed in bfloat16 or wider, within the bound.
A program may use at most 64 MiB of HBM per device.

```python
import math
import jax
import jax.numpy as jnp
import numpy as np
from jax import lax

DH = 128
HEADS = 16
KVH = 2
STRETCHES = 8
SEQ = 16384
PIECES = 32
BLOCK = 64
MOSTDOC = 2048
NDOCS = 32


def draw_queries(key, part):
    base_key = jax.random.fold_in(key, 1)
    base = jax.random.truncated_normal(base_key, -4.0, 4.0, (SEQ, HEADS * DH), jnp.float32)
    return base.astype(jnp.bfloat16)


def draw_keys(key, part):
    base_key = jax.random.fold_in(key, 2)
    base = jax.random.truncated_normal(base_key, -4.0, 4.0, (SEQ, KVH * DH), jnp.float32)
    return base.astype(jnp.bfloat16)


def draw_head_map(key, part):
    order = jax.random.permutation(jax.random.fold_in(key, 3), HEADS)
    return (order % KVH).astype(jnp.int32)


def draw_plan(key, part):
    row_keys = jax.random.split(jax.random.fold_in(key, 5), STRETCHES)
    rows = jax.vmap(lambda row_key: jax.random.permutation(row_key, PIECES))(row_keys)
    return rows.astype(jnp.int32)


def shard_levels(own_key, dims, cuts, low, high):
    level, own = 1.0, jax.random.fold_in(own_key, 6)
    for axis_at, shards_of in cuts:
        steps = jnp.exp(jax.random.uniform(jax.random.fold_in(own, axis_at), (shards_of,), jnp.float32, low / len(cuts), high / len(cuts)))
        level = level * jnp.repeat(steps, dims[axis_at] // shards_of).reshape([-1 if axis == axis_at else 1 for axis in range(len(dims))])
    return level


def length_profile(count, total, reach, skew):
    portions = [(1 << 20) // math.isqrt(rank ** skew) + 1 for rank in range(2, count + 1)]
    surplus, given = total - reach - (count - 1), [1] * (count - 1)
    while surplus > 0:
        movable = [i for i in range(count - 1) if given[i] < reach]
        mass, left = sum([portions[i] for i in movable]), surplus
        for i in movable:
            extra = min(reach - given[i], max(1, left * portions[i] // mass), surplus)
            given[i] = given[i] + extra
            surplus = surplus - extra
    return np.array([reach] + given)


def uneven(key, amount, total, limit, lean):
    if amount == 2:
        one = jax.random.randint(key, (), max(1, total - limit), min(limit, total - 1) + 1)
        return jnp.stack([one, total - one])
    tallies = jnp.asarray(length_profile(amount, total, limit, lean), jnp.int32)
    twos = (amount - 1) // 2
    source_of, sink = tallies[1:1 + 2 * twos:2], tallies[2:2 + 2 * twos:2]
    room = jnp.minimum(source_of - 1, limit - sink)
    moved = jax.random.randint(jax.random.fold_in(key, 1), (twos,), 0, 1 << 20) % (room + 1)
    tallies = tallies.at[1:1 + 2 * twos:2].set(source_of - moved).at[2:2 + 2 * twos:2].set(sink + moved)
    return tallies[jax.random.permutation(jax.random.fold_in(key, 2), amount)]


def bell_draw(key, extent, spread, reach, cuts=(), kind=jnp.bfloat16):
    values = jax.random.normal(key, extent, jnp.float32) * spread
    if len(cuts) > 0:
        values = shard_levels(key, extent, cuts, -0.22, 0.18) * values
    return jnp.clip(values, min=-reach, max=reach).astype(kind)


def setup_inputs(seed: int = 0, part: int = 0) -> dict:
    splits = jax.random.split(jax.random.key(seed), 7)
    own_keys = jax.random.split(jax.random.fold_in(splits[6], part), 7)
    queries = draw_queries(jax.random.fold_in(jax.random.fold_in(splits[6], part), 71), part)
    keys = draw_keys(jax.random.fold_in(jax.random.fold_in(splits[6], part), 71), part)
    values = bell_draw(own_keys[2], (SEQ, KVH * DH), 1.0, 6.0, ((0, 128),))
    head_map = draw_head_map(jax.random.fold_in(jax.random.fold_in(splits[6], part), 71), part)
    doc_lengths = uneven(splits[4], NDOCS, SEQ, MOSTDOC, 2).astype(jnp.int32)
    plan = draw_plan(jax.random.fold_in(splits[6], 71), part)
    return dict(queries=queries, keys=keys, values=values, head_map=head_map, doc_lengths=doc_lengths, plan=plan)


def reference(queries, keys, values, head_map, doc_lengths, plan):
    seq_rows = queries.shape[0]
    query_rows = queries.reshape(seq_rows, HEADS, DH)
    key_rows = keys.reshape(seq_rows, KVH, DH)[:, head_map]
    value_rows = values.reshape(seq_rows, KVH, DH)[:, head_map]
    doc_ends = jnp.cumsum(doc_lengths).astype(jnp.int32)
    positions = jnp.arange(seq_rows, dtype=jnp.int32)
    doc_of = lax.optimization_barrier(jnp.sum((positions[:, None] >= doc_ends[None, :]).astype(jnp.int32), axis=1)).astype(jnp.int32)
    tile = math.gcd(256, seq_rows)
    span = MOSTDOC + tile
    key_padded = jnp.pad(key_rows, ((MOSTDOC, 0), (0, 0), (0, 0)))
    value_padded = jnp.pad(value_rows, ((MOSTDOC, 0), (0, 0), (0, 0)))
    doc_padded = jnp.concatenate([jnp.full((MOSTDOC,), -1, jnp.int32), doc_of])
    scale = 1.0 / math.sqrt(DH)

    def one_tile(tile_index):
        first = (tile_index * tile).astype(jnp.int32)
        query_tile = lax.dynamic_slice_in_dim(query_rows, first, tile, 0).astype(jnp.float32)
        key_tile = lax.dynamic_slice_in_dim(key_padded, first, span, 0).astype(jnp.float32)
        value_tile = lax.dynamic_slice_in_dim(value_padded, first, span, 0).astype(jnp.float32)
        query_doc = lax.dynamic_slice_in_dim(doc_of, first, tile, 0)
        key_doc = lax.dynamic_slice_in_dim(doc_padded, first, span, 0)
        query_pos = first + jnp.arange(tile, dtype=jnp.int32)
        key_pos = first - MOSTDOC + jnp.arange(span, dtype=jnp.int32)
        visible = (query_doc[:, None] == key_doc[None, :]) & (key_pos[None, :] <= query_pos[:, None])
        scores = jnp.einsum('thd,shd->ths', query_tile, key_tile) * scale
        scores = jnp.where(visible[:, None, :], scores, -jnp.inf)
        top = lax.optimization_barrier(jnp.max(scores, axis=-1))
        expo = jnp.exp(scores - top[..., None])
        total = lax.optimization_barrier(jnp.sum(expo, axis=-1))
        weights = lax.optimization_barrier(expo.astype(jnp.bfloat16)).astype(jnp.float32)
        summed = jnp.einsum('ths,shd->thd', weights, value_tile)
        return (summed / total[..., None]).astype(jnp.bfloat16)
    attended = lax.map(one_tile, jnp.arange(seq_rows // tile, dtype=jnp.int32))
    attended = attended.reshape(STRETCHES, PIECES, BLOCK, HEADS * DH)
    picked = attended[jnp.arange(STRETCHES, dtype=jnp.int32)[:, None], plan]
    picked = picked.reshape(STRETCHES, STRETCHES, PIECES // STRETCHES, BLOCK, HEADS * DH)
    return jnp.swapaxes(picked, 0, 1).reshape(seq_rows, HEADS * DH)
```

```python
import functools
import math

import jax
import jax.numpy as jnp
from jax import lax
from jax.experimental import pallas as pl
from jax.experimental.pallas import tpu as pltpu
from jax.sharding import PartitionSpec as P

DH = 128
MESH = pl.DeviceIdType.MESH
VMEM = pltpu.VMEM
SMEM = pltpu.SMEM
NEG = -1e30


def slot_of(head_map, h, heads, kv_heads):
    per = heads // kv_heads
    mine = head_map[h]
    before = jnp.int32(0)
    for g in range(h):
        before += (head_map[g] == mine).astype(jnp.int32)
    return mine * per + before


def spread_kernel(nb, nz, hm, q, k, v, qo, kvo, sq, skv, rq, rkv, sems):
    b, u = lax.axis_index("blk"), lax.axis_index("uly")
    heads = hm.shape[0]
    tokens = q.shape[0]
    kvh = k.shape[1] // DH
    part = tokens // nb
    (s1q_s, s1q_r, s1k_s, s1k_r, s2q_s, s2q_r, s2c_s, s2c_r, s2p_s, s2p_r, gy_s, gy_r, gc_s, gc_r) = sems

    barrier = pltpu.get_barrier_semaphore()
    for d in range(1, nb):
        pl.semaphore_signal(barrier, inc=1, device_id={"blk": lax.rem(b + d, nb)}, device_id_type=MESH)
    for d in range(1, nz):
        pl.semaphore_signal(barrier, inc=1, device_id={"uly": lax.rem(u + d, nz)}, device_id_type=MESH)

    slots = [slot_of(hm, h, heads, kvh) for h in range(heads)]

    def head_at(i):
        at = jnp.int32(0)
        for h in range(heads):
            at += h * (slots[h] == i).astype(jnp.int32)
        return at

    for i in range(nb):
        for e in range(kvh):
            skv[i, e, 0] = k[i * part : (i + 1) * part, e * DH : (e + 1) * DH]
            skv[i, e, 1] = v[i * part : (i + 1) * part, e * DH : (e + 1) * DH]

    pl.semaphore_wait(barrier, nb - 1 + nz - 1)

    s1k, s1q = [], []
    for d in list(range(1, nb)) + [0]:
        to = lax.rem(b + d, nb)
        if d == 0:
            c = pltpu.make_async_copy(skv.at[to], rkv.at[b], s1k_r.at[b])
        else:
            c = pltpu.make_async_remote_copy(
                src_ref=skv.at[to], dst_ref=rkv.at[b], send_sem=s1k_s.at[d], recv_sem=s1k_r.at[b],
                device_id={"blk": to}, device_id_type=MESH)
        c.start()
        s1k.append((d, c))
    for d in list(range(1, nb)) + [0]:
        to = lax.rem(b + d, nb)
        for e in range(kvh):
            sq[to, e] = q[:, pl.ds(head_at(e * nb + to) * DH, DH)]
        if d == 0:
            c = pltpu.make_async_copy(sq.at[to], rq.at[b], s1q_r.at[b])
        else:
            c = pltpu.make_async_remote_copy(
                src_ref=sq.at[to], dst_ref=rq.at[b], send_sem=s1q_s.at[d], recv_sem=s1q_r.at[b],
                device_id={"blk": to}, device_id_type=MESH)
        c.start()
        s1q.append((d, c))

    def arrived(dst, sem):
        pltpu.make_async_copy(dst, dst, sem).wait()

    for s in range(nb):
        arrived(rkv.at[s], s1k_r.at[s])

    zorder = [0]
    for d in range(1, nz // 2 + 1):
        zorder += [d] if d == nz - d else [d, nz - d]
    zorder = zorder[1:][::-1] + [0]
    sent = []
    for d in zorder:
        to = lax.rem(u + d, nz)
        s, e = to // kvh, lax.rem(to, kvh)
        prior = lax.rem(s + nb - 1, nb)
        for cp, src_s, ss, rs in ((1, s, s2c_s, s2c_r), (0, prior, s2p_s, s2p_r)):
            src, dst = rkv.at[src_s, e], kvo.at[:, cp * nz + u, b]
            if d == 0:
                c = pltpu.make_async_copy(src, dst, rs.at[u])
            else:
                c = pltpu.make_async_remote_copy(
                    src_ref=src, dst_ref=dst, send_sem=ss.at[d], recv_sem=rs.at[u],
                    device_id={"uly": to}, device_id_type=MESH)
            c.start()
            sent.append((d, c))
    for s in range(nb):
        arrived(rq.at[s], s1q_r.at[s])
    for d in zorder:
        to = lax.rem(u + d, nz)
        s, e = to // kvh, lax.rem(to, kvh)
        if d == 0:
            c = pltpu.make_async_copy(rq.at[s, e], qo.at[u], s2q_r.at[u])
        else:
            c = pltpu.make_async_remote_copy(
                src_ref=rq.at[s, e], dst_ref=qo.at[u], send_sem=s2q_s.at[d], recv_sem=s2q_r.at[u],
                device_id={"uly": to}, device_id_type=MESH)
        c.start()
        sent.append((d, c))

    for z in range(nz):
        arrived(kvo.at[:, nz + z, b], s2c_r.at[z])
        arrived(kvo.at[:, z, b], s2p_r.at[z])

    other = b + 1 - 2 * lax.rem(b, 2)
    mine = kvo.at[:, :, b]
    for d in range(1, nb // 2):
        c = pltpu.make_async_remote_copy(
            src_ref=mine, dst_ref=mine, send_sem=gy_s.at[d], recv_sem=gy_r.at[d],
            device_id={"blk": lax.rem(b + 2 * d, nb)}, device_id_type=MESH)
        c.start()
        sent.append((1, c))
    for d in range(nb // 2):
        at = lax.rem(b + nb - 2 * d, nb)
        block = kvo.at[:, :, at]
        if d > 0:
            arrived(block, gy_r.at[d])
        c = pltpu.make_async_remote_copy(
            src_ref=block, dst_ref=block, send_sem=gc_s.at[d], recv_sem=gc_r.at[d],
            device_id={"blk": other}, device_id_type=MESH)
        c.start()
        sent.append((1, c))
    for d in range(nb // 2):
        arrived(kvo.at[:, :, lax.rem(other + nb - 2 * d, nb)], gc_r.at[d])
    for z in range(nz):
        arrived(qo.at[z], s2q_r.at[z])
    for d, c in s1k + s1q + sent:
        if d != 0:
            c.wait_send()


def attend_kernel(nz, kvh, tile, chunk, lengths, q, k, v, o, lo_t):
    stretch = q.shape[0]
    s = lax.axis_index("uly") // kvh
    base = (s - 1) * stretch
    lanes = lo_t.shape[0]
    rows = stretch // lanes
    pos = lax.broadcasted_iota(jnp.int32, (lanes, lanes), 0) * lanes + lax.broadcasted_iota(
        jnp.int32, (lanes, lanes), 1) + s * stretch
    first = jnp.zeros((lanes, lanes), jnp.int32)
    start = jnp.int32(0)
    for n in range(lengths.shape[0]):
        first = jnp.where(pos >= start, start, first)
        start = start + lengths[n]
    lo_t[...] = jnp.transpose((first - base).astype(jnp.float32))
    scale = math.log2(math.e) / math.sqrt(DH)
    ones = jnp.ones((chunk, DH), jnp.bfloat16)

    def one_tile(t, _):
        row0 = t * tile
        qt = q[pl.ds(row0, tile), :]
        lane = lax.broadcasted_iota(jnp.int32, (lanes, lanes), 1)
        cols = [
            jnp.sum(jnp.where(lane == t * (tile // lanes) + i, lo_t[...], 0.0), axis=1, keepdims=True)
            for i in range(tile // lanes)
        ]
        lo = jnp.concatenate(cols, axis=0).astype(jnp.int32)
        p0 = s * stretch + row0
        begin = jnp.int32(0)
        at = jnp.int32(0)
        for n in range(lengths.shape[0]):
            begin = jnp.where(p0 >= at, at, begin)
            at = at + lengths[n]
        lowest = (begin - base) // chunk
        last = (stretch + row0 + tile + chunk - 1) // chunk
        hi = stretch + row0 + lax.broadcasted_iota(jnp.int32, (tile, 1), 0)

        def key_step(c, carry):
            m, acc = carry
            kt = k[pl.ds(c * chunk, chunk), :]
            vt = v[pl.ds(c * chunk, chunk), :]
            sc = lax.dot_general(qt, kt, (((1,), (1,)), ((), ())), preferred_element_type=jnp.float32)
            key = c * chunk + lax.broadcasted_iota(jnp.int32, (tile, chunk), 1)
            sc = jnp.where((key >= lo) & (key <= hi), sc, NEG)
            new_m = jnp.maximum(m, jnp.max(sc, axis=1, keepdims=True))
            p = jnp.where(sc <= NEG, 0.0, jnp.exp2((sc - new_m) * scale))
            alpha = jnp.exp2((m - new_m) * scale)
            both = jnp.concatenate([vt, ones], axis=1)
            acc = acc * alpha + jnp.dot(p.astype(jnp.bfloat16), both, preferred_element_type=jnp.float32)
            return new_m, acc

        m, acc = lax.fori_loop(
            lowest, last, key_step,
            (jnp.full((tile, 1), NEG, jnp.float32), jnp.zeros((tile, 2 * DH), jnp.float32)))
        o[pl.ds(row0, tile), :] = (acc[:, :DH] / acc[:, DH:]).astype(jnp.bfloat16)
        return 0

    lax.fori_loop(0, stretch // tile, one_tile, 0)


def return_kernel(nb, nz, kvh, hm, plan, a, o, sa, ra, ss, rs):
    b, u = lax.axis_index("blk"), lax.axis_index("uly")
    s, e = u // kvh, lax.rem(u, kvh)
    heads = hm.shape[0]
    pieces = a.shape[0]
    per = pieces // (nb * kvh)
    barrier = pltpu.get_barrier_semaphore()
    peers = [(d, f) for f in range(kvh) for d in range(nb) if (d, f) != (0, 0)]

    def where(d, f):
        return {"blk": lax.rem(b + d, nb), "uly": s * kvh + lax.rem(e + f, kvh)}

    for d, f in peers:
        pl.semaphore_signal(barrier, inc=1, device_id=where(d, f), device_id_type=MESH)
    for i in range(pieces):
        sa[i] = a[plan[s, i]]
    pl.semaphore_wait(barrier, len(peers))
    slot = e * nb + b
    copies = []
    for d, f in peers + [(0, 0)]:
        to = where(d, f)
        src = sa.at[pl.ds((to["blk"] * kvh + to["uly"] - s * kvh) * per, per)]
        if (d, f) == (0, 0):
            pltpu.make_async_copy(src, ra.at[slot], rs.at[slot]).start()
        else:
            c = pltpu.make_async_remote_copy(
                src_ref=src, dst_ref=ra.at[slot], send_sem=ss.at[d * kvh + f], recv_sem=rs.at[slot],
                device_id=to, device_id_type=MESH)
            c.start()
            copies.append(c)
    for i in range(heads):
        pltpu.make_async_copy(ra.at[i], ra.at[i], rs.at[i]).wait()
    for h in range(heads):
        o[:, h * DH : (h + 1) * DH] = ra[slot_of(hm, h, heads, kvh)].reshape(o.shape[0], DH)
    for c in copies:
        c.wait_send()


def body(queries, keys, values, head_map, doc_lengths, plan):
    nb, nz = lax.axis_size("blk"), lax.axis_size("uly")
    tokens = queries.shape[0]
    kvh = keys.shape[1] // DH
    stretch = tokens * nz
    part = tokens // nb
    heads = head_map.shape[0]
    pieces = plan.shape[1]
    block = stretch // pieces
    bf = jnp.bfloat16
    dma = pltpu.SemaphoreType.DMA
    vm = pl.BlockSpec(memory_space=VMEM)
    sm = pl.BlockSpec(memory_space=SMEM)

    qs, kvs = pl.pallas_call(
        functools.partial(spread_kernel, nb, nz),
        out_shape=(
            jax.ShapeDtypeStruct((nz, tokens, DH), bf),
            jax.ShapeDtypeStruct((2, 2 * nz, nb, part, DH), bf),
        ),
        in_specs=[sm, vm, vm, vm],
        out_specs=(vm, vm),
        scratch_shapes=[
            VMEM((nb, kvh, tokens, DH), bf),
            VMEM((nb, kvh, 2, part, DH), bf),
            VMEM((nb, kvh, tokens, DH), bf),
            VMEM((nb, kvh, 2, part, DH), bf),
            [dma((n,)) for n in (nb, nb, nb, nb, nz, nz, nz, nz, nz, nz, nb // 2, nb // 2, nb // 2, nb // 2)],
        ],
        compiler_params=pltpu.CompilerParams(collective_id=0, has_side_effects=True, vmem_limit_bytes=40 << 20),
        name="spread",
    )(head_map, queries, keys, values)

    attended = pl.pallas_call(
        functools.partial(attend_kernel, nz, kvh, 256, 512),
        out_shape=jax.ShapeDtypeStruct((stretch, DH), bf),
        in_specs=[sm, vm, vm, vm],
        out_specs=vm,
        scratch_shapes=[VMEM((128, 128), jnp.float32)],
        compiler_params=pltpu.CompilerParams(vmem_limit_bytes=40 << 20),
        name="attend",
    )(doc_lengths, qs.reshape(stretch, DH), kvs[0].reshape(2 * stretch, DH), kvs[1].reshape(2 * stretch, DH))

    return pl.pallas_call(
        functools.partial(return_kernel, nb, nz, kvh),
        out_shape=jax.ShapeDtypeStruct((tokens, heads * DH), bf),
        in_specs=[sm, sm, vm],
        out_specs=vm,
        scratch_shapes=[
            VMEM((pieces, block, DH), bf),
            VMEM((heads, tokens // block, block, DH), bf),
            dma((heads,)),
            dma((heads,)),
        ],
        compiler_params=pltpu.CompilerParams(collective_id=1, has_side_effects=True, vmem_limit_bytes=40 << 20),
        name="give_back",
    )(head_map, plan, attended.reshape(pieces, block, DH))


def solution(mesh):
    return jax.shard_map(
        body,
        mesh=mesh,
        in_specs=(
            P(("blk", "uly"), "tp"),
            P(("blk", "uly"), "tp"),
            P(("blk", "uly"), "tp"),
            P("tp"),
            P(),
            P(),
        ),
        out_specs=P(("blk", "uly"), "tp"),
        check_vma=False,
    )
```

```python
import functools
import math

import jax
import jax.numpy as jnp
from jax import lax
from jax.experimental import pallas as pl
from jax.experimental.pallas import tpu as pltpu
from jax.sharding import PartitionSpec as P

DH = 128
MESH = pl.DeviceIdType.MESH
VMEM = pltpu.VMEM
SMEM = pltpu.SMEM
NEG = -1e30


def slot_of(head_map, h, heads, kv_heads):
    per = heads // kv_heads
    mine = head_map[h]
    before = jnp.int32(0)
    for g in range(h):
        before += (head_map[g] == mine).astype(jnp.int32)
    return mine * per + before


def fused_kernel(nb, nz, hm, lengths, plan, q_hbm, k_hbm, v_hbm, o, q, sq, skv, rq, rkv, qo, kvo, att, sa, ra, lo_t, sc, sems):
    b, u = lax.axis_index("blk"), lax.axis_index("uly")
    heads = hm.shape[0]
    tokens = q.shape[0]
    kvh = skv.shape[1]
    pieces = att.shape[0]
    per = pieces // (nb * kvh)
    stretch = tokens * nz
    window = nz + 1
    (s1q_s, s1q_r, s1k_s, s1k_r, s2q_s, s2q_r, s2c_s, s2c_r, s2p_s, s2p_r, gy_s, gy_r, gc_s, gc_r, rt_s, rt_r, in_s) = sems
    my_s, my_e = u // kvh, lax.rem(u, kvh)

    def remote(src, dst, ss, rs, **to):
        return pltpu.make_async_remote_copy(
            src_ref=src, dst_ref=dst, send_sem=ss, recv_sem=rs, device_id=to, device_id_type=MESH)

    def arrived(dst, sem):
        pltpu.make_async_copy(dst, dst, sem).wait()

    loads = []
    for e in range(kvh):
        for i, ref in enumerate((k_hbm, v_hbm)):
            c = pltpu.make_async_copy(ref.at[:, :, e * DH : (e + 1) * DH], skv.at[:, e, i], in_s.at[2 * e + i])
            c.start()
            loads.append(c)
    load_q = pltpu.make_async_copy(q_hbm, q, in_s.at[2 * kvh])
    load_q.start()

    barrier = pltpu.get_barrier_semaphore()
    twin = [(d, f) for f in range(1, kvh) for d in range(1, nb)]
    for d in range(1, nb):
        pl.semaphore_signal(barrier, inc=1, device_id={"blk": lax.rem(b + d, nb)}, device_id_type=MESH)
    for d in range(1, nz):
        pl.semaphore_signal(barrier, inc=1, device_id={"uly": lax.rem(u + d, nz)}, device_id_type=MESH)
    for d, f in twin:
        pl.semaphore_signal(
            barrier, inc=1, device_id={"blk": lax.rem(b + d, nb), "uly": my_s * kvh + lax.rem(my_e + f, kvh)},
            device_id_type=MESH)
    for c in loads:
        c.wait()
    pl.semaphore_wait(barrier, nb - 1 + nz - 1 + len(twin))

    sent = []
    near = []
    for d in range(1, nb // 2 + 1):
        near += [d] if d == nb - d else [d, nb - d]
    for d in near + [0]:
        to = lax.rem(b + d, nb)
        if d == 0:
            pltpu.make_async_copy(skv.at[to], rkv.at[b], s1k_r.at[b]).start()
        else:
            c = remote(skv.at[to], rkv.at[b], s1k_s.at[d], s1k_r.at[b], blk=to)
            c.start()
            sent.append(c)
    slots = [slot_of(hm, h, heads, kvh) for h in range(heads)]

    def head_at(i):
        at = jnp.int32(0)
        for h in range(heads):
            at += h * (slots[h] == i).astype(jnp.int32)
        return at

    load_q.wait()
    for d in near + [0]:
        to = lax.rem(b + d, nb)
        for e in range(kvh):
            sq[to, e] = q[:, pl.ds(head_at(e * nb + to) * DH, DH)]
        if d == 0:
            pltpu.make_async_copy(sq.at[to], rq.at[b], s1q_r.at[b]).start()
        else:
            c = remote(sq.at[to], rq.at[b], s1q_s.at[d], s1q_r.at[b], blk=to)
            c.start()
            sent.append(c)
    for s in range(nb):
        arrived(rkv.at[s], s1k_r.at[s])

    znear = []
    for d in range(1, nz // 2 + 1):
        znear += [d] if d == nz - d else [d, nz - d]
    for cp, ss, rs in ((1, s2c_s, s2c_r), (0, s2p_s, s2p_r)):
        for d in znear + [0]:
            to = lax.rem(u + d, nz)
            s, e = to // kvh, lax.rem(to, kvh)
            src = rkv.at[s if cp else lax.rem(s + nb - 1, nb), e]
            dst = kvo.at[:, cp * nz + u, b]
            if d == 0:
                pltpu.make_async_copy(src, dst, rs.at[u]).start()
            else:
                c = remote(src, dst, ss.at[d], rs.at[u], uly=to)
                c.start()
                sent.append(c)
    for s in range(nb):
        arrived(rq.at[s], s1q_r.at[s])
    for d in znear + [0]:
        to = lax.rem(u + d, nz)
        s, e = to // kvh, lax.rem(to, kvh)
        if d == 0:
            pltpu.make_async_copy(rq.at[s, e], qo.at[u], s2q_r.at[u]).start()
        else:
            c = remote(rq.at[s, e], qo.at[u], s2q_s.at[d], s2q_r.at[u], uly=to)
            c.start()
            sent.append(c)

    row = lax.broadcasted_iota(jnp.int32, (tokens, tokens), 0)
    pos = row * tokens + lax.broadcasted_iota(jnp.int32, (tokens, tokens), 1) + my_s * stretch
    first = jnp.zeros((tokens, tokens), jnp.int32)
    start = jnp.int32(0)
    for n in range(lengths.shape[0]):
        first = jnp.where(pos >= start, start, first)
        start = start + lengths[n]
    lo_t[...] = jnp.transpose((first - (my_s - 1) * stretch - row * tokens).astype(jnp.float32))

    other = b + 1 - 2 * lax.rem(b, 2)
    half = nb // 2
    for cp, rs in ((1, s2c_r), (0, s2p_r)):
        for z in range(nz):
            arrived(kvo.at[:, cp * nz + z, b], rs.at[z])
        mine = kvo.at[:, cp * nz : (cp + 1) * nz, b]
        for d in range(1, half):
            c = remote(mine, mine, gy_s.at[cp * half + d], gy_r.at[cp * half + d], blk=lax.rem(b + 2 * d, nb))
            c.start()
            sent.append(c)
        c = remote(mine, mine, gc_s.at[cp * half], gc_r.at[cp * half], blk=other)
        c.start()
        sent.append(c)
    for cp in (1, 0):
        for d in range(1, half):
            block = kvo.at[:, cp * nz : (cp + 1) * nz, lax.rem(b + nb - 2 * d, nb)]
            arrived(block, gy_r.at[cp * half + d])
            c = remote(block, block, gc_s.at[cp * half + d], gc_r.at[cp * half + d], blk=other)
            c.start()
            sent.append(c)
    for cp in (1, 0):
        for d in range(half):
            arrived(kvo.at[:, cp * nz : (cp + 1) * nz, lax.rem(other + nb - 2 * d, nb)], gc_r.at[cp * half + d])

    scale = math.log2(math.e) / math.sqrt(DH)
    chunks = [(c, min(2, window - c)) for c in range(0, window, 2)]

    def one_tile(i, _):
        d = jnp.where(lax.rem(i, 2) == 1, (i + 1) // 2, nz - i // 2)
        z = lax.rem(u + d, nz)
        arrived(qo.at[z], s2q_r.at[z])
        qt = qo[z]
        lane = lax.broadcasted_iota(jnp.int32, (tokens, tokens), 1)
        lo = jnp.sum(jnp.where(lane == z, lo_t[...], 0.0), axis=1, keepdims=True).astype(jnp.int32)
        lo = jnp.broadcast_to(lo, (tokens, tokens))
        causal = lane <= lax.broadcasted_iota(jnp.int32, (tokens, tokens), 0)
        top = jnp.full((tokens, tokens), NEG, jnp.float32)
        for c, n in chunks:
            kt = kvo[0, pl.ds(z + c, n)].reshape(n * tokens, DH)
            s = lax.dot_general(qt, kt, (((1,), (1,)), ((), ())), preferred_element_type=jnp.float32)
            for j in range(n):
                seen = lane >= lo - (c + j) * tokens
                if c + j == window - 1:
                    seen = seen & causal
                sj = jnp.where(seen, s[:, j * tokens : (j + 1) * tokens], NEG)
                sc[:, (c + j) * tokens : (c + j + 1) * tokens] = sj
                top = jnp.maximum(top, sj)
        m = jnp.max(top, axis=1, keepdims=True)
        acc = jnp.zeros((tokens, 2 * DH), jnp.float32)
        for c, n in chunks:
            p = jnp.exp2((sc[:, c * tokens : (c + n) * tokens] - m) * scale).astype(jnp.bfloat16)
            vt = kvo[1, pl.ds(z + c, n)].reshape(n * tokens, DH)
            both = jnp.concatenate([vt, jnp.ones_like(vt)], axis=1)
            acc = acc + jnp.dot(p, both, preferred_element_type=jnp.float32)
        out = (acc[:, :DH] / acc[:, DH:]).astype(jnp.bfloat16)
        att[pl.ds(z * (tokens // att.shape[1]), tokens // att.shape[1])] = out.reshape(tokens // att.shape[1], att.shape[1], DH)
        return 0

    lax.fori_loop(0, nz, one_tile, 0)

    for i in range(pieces):
        sa[i] = att[plan[my_s, i]]
    slot = my_e * nb + b
    for d, f in [(d, f) for f in range(kvh) for d in near] + [(0, f) for f in range(kvh - 1, -1, -1)]:
        tb, te = lax.rem(b + d, nb), lax.rem(my_e + f, kvh)
        src = sa.at[pl.ds((tb * kvh + te) * per, per)]
        if (d, f) == (0, 0):
            pltpu.make_async_copy(src, ra.at[slot], rt_r.at[slot]).start()
        else:
            c = remote(src, ra.at[slot], rt_s.at[d * kvh + f], rt_r.at[slot], blk=tb, uly=my_s * kvh + te)
            c.start()
            sent.append(c)
    for i in range(heads):
        arrived(ra.at[i], rt_r.at[i])
    for h in range(heads):
        o[:, h * DH : (h + 1) * DH] = ra[slot_of(hm, h, heads, kvh)].reshape(tokens, DH)
    for c in sent:
        c.wait_send()


def body(queries, keys, values, head_map, doc_lengths, plan):
    nb, nz = lax.axis_size("blk"), lax.axis_size("uly")
    tokens = queries.shape[0]
    kvh = keys.shape[1] // DH
    stretch = tokens * nz
    part = tokens // nb
    heads = head_map.shape[0]
    pieces = plan.shape[1]
    block = stretch // pieces
    bf = jnp.bfloat16
    dma = pltpu.SemaphoreType.DMA
    sm = pl.BlockSpec(memory_space=SMEM)
    hbm = pl.BlockSpec(memory_space=pl.ANY)
    return pl.pallas_call(
        functools.partial(fused_kernel, nb, nz),
        out_shape=jax.ShapeDtypeStruct((tokens, heads * DH), bf),
        in_specs=[sm, sm, sm, hbm, hbm, hbm],
        out_specs=pl.BlockSpec(memory_space=VMEM),
        scratch_shapes=[
            VMEM((tokens, heads * DH), bf),
            VMEM((nb, kvh, tokens, DH), bf),
            VMEM((nb, kvh, 2, part, DH), bf),
            VMEM((nb, kvh, tokens, DH), bf),
            VMEM((nb, kvh, 2, part, DH), bf),
            VMEM((nz, tokens, DH), bf),
            VMEM((2, 2 * nz, nb, part, DH), bf),
            VMEM((pieces, block, DH), bf),
            VMEM((pieces, block, DH), bf),
            VMEM((heads, tokens // block, block, DH), bf),
            VMEM((tokens, tokens), jnp.float32),
            VMEM((tokens, (nz + 1) * tokens), jnp.float32),
            [dma((n,)) for n in (nb, nb, nb, nb, nz, nz, nz, nz, nz, nz, nb, nb, nb, nb, heads, heads, 2 * kvh + 1)],
        ],
        compiler_params=pltpu.CompilerParams(collective_id=0, has_side_effects=True, vmem_limit_bytes=63 << 20),
        name="fused",
    )(head_map, doc_lengths, plan, queries, keys.reshape(nb, part, kvh * DH), values.reshape(nb, part, kvh * DH))


def solution(mesh):
    return jax.shard_map(
        body,
        mesh=mesh,
        in_specs=(
            P(("blk", "uly"), "tp"),
            P(("blk", "uly"), "tp"),
            P(("blk", "uly"), "tp"),
            P("tp"),
            P(),
            P(),
        ),
        out_specs=P(("blk", "uly"), "tp"),
        check_vma=False,
    )
```

```python
import functools
import math

import jax
import jax.numpy as jnp
from jax import lax
from jax.experimental import pallas as pl
from jax.experimental.pallas import tpu as pltpu
from jax.sharding import PartitionSpec as P

DH = 128
MESH = pl.DeviceIdType.MESH
VMEM = pltpu.VMEM
SMEM = pltpu.SMEM
NEG = -1e30


def slot_of(head_map, h, heads, kv_heads):
    per = heads // kv_heads
    mine = head_map[h]
    before = jnp.int32(0)
    for g in range(h):
        before += (head_map[g] == mine).astype(jnp.int32)
    return mine * per + before


def fused_kernel(nb, nz, hm, lengths, plan, q_hbm, k_hbm, v_hbm, o, q, sq, skv, rq, rkv, qo, kvo, att, sa, ra, lo_t, sc, sems):
    b, u = lax.axis_index("blk"), lax.axis_index("uly")
    heads = hm.shape[0]
    tokens = q.shape[0]
    kvh = skv.shape[1]
    pieces = att.shape[0]
    per = pieces // (nb * kvh)
    stretch = tokens * nz
    window = nz + 1
    (s1q_s, s1q_r, s1k_s, s1k_r, s2q_s, s2q_r, s2c_s, s2c_r, s2p_s, s2p_r, gy_s, gy_r, gc_s, gc_r, rt_s, rt_r, in_s) = sems
    my_s, my_e = u // kvh, lax.rem(u, kvh)

    def remote(src, dst, ss, rs, **to):
        return pltpu.make_async_remote_copy(
            src_ref=src, dst_ref=dst, send_sem=ss, recv_sem=rs, device_id=to, device_id_type=MESH)

    def arrived(dst, sem):
        pltpu.make_async_copy(dst, dst, sem).wait()

    barrier = pltpu.get_barrier_semaphore()
    twin = [(d, f) for f in range(1, kvh) for d in range(1, nb)]
    for d in range(1, nb):
        pl.semaphore_signal(barrier, inc=1, device_id={"blk": lax.rem(b + d, nb)}, device_id_type=MESH)
    for d in range(1, nz):
        pl.semaphore_signal(barrier, inc=1, device_id={"uly": lax.rem(u + d, nz)}, device_id_type=MESH)
    for d, f in twin:
        pl.semaphore_signal(
            barrier, inc=1, device_id={"blk": lax.rem(b + d, nb), "uly": my_s * kvh + lax.rem(my_e + f, kvh)},
            device_id_type=MESH)
    loads = []
    for e in range(kvh):
        for i, ref in enumerate((k_hbm, v_hbm)):
            c = pltpu.make_async_copy(ref.at[:, :, e * DH : (e + 1) * DH], skv.at[:, e, i], in_s.at[2 * e + i])
            c.start()
            loads.append(c)
    load_q = pltpu.make_async_copy(q_hbm, q, in_s.at[2 * kvh])
    load_q.start()

    slots = [slot_of(hm, h, heads, kvh) for h in range(heads)]

    def head_at(i):
        at = jnp.int32(0)
        for h in range(heads):
            at += h * (slots[h] == i).astype(jnp.int32)
        return at

    def pack(to):
        for e in range(kvh):
            sq[to, e] = q[:, pl.ds(head_at(e * nb + to) * DH, DH)]

    near = []
    for d in range(1, nb // 2 + 1):
        near += [d] if d == nb - d else [d, nb - d]
    for c in loads:
        c.wait()
    load_q.wait()
    for d in [0] + near:
        pack(lax.rem(b + d, nb))
    pl.semaphore_wait(barrier, nb - 1 + nz - 1 + len(twin))

    sent = []
    for d in near:
        to = lax.rem(b + d, nb)
        c = remote(skv.at[to], rkv.at[b], s1k_s.at[d], s1k_r.at[b], blk=to)
        c.start()
        sent.append(c)
    pltpu.make_async_copy(skv.at[b], rkv.at[b], s1k_r.at[b]).start()
    for d in near:
        to = lax.rem(b + d, nb)
        c = remote(sq.at[to], rq.at[b], s1q_s.at[d], s1q_r.at[b], blk=to)
        c.start()
        sent.append(c)
    pltpu.make_async_copy(sq.at[b], rq.at[b], s1q_r.at[b]).start()
    for s in range(nb):
        arrived(rkv.at[s], s1k_r.at[s])

    znear = []
    for d in range(1, nz // 2 + 1):
        znear += [d] if d == nz - d else [d, nz - d]
    for cp, ss, rs in ((1, s2c_s, s2c_r), (0, s2p_s, s2p_r)):
        for d in znear + [0]:
            to = lax.rem(u + d, nz)
            s, e = to // kvh, lax.rem(to, kvh)
            src = rkv.at[s if cp else lax.rem(s + nb - 1, nb), e]
            dst = kvo.at[:, cp * nz + u, b]
            if d == 0:
                pltpu.make_async_copy(src, dst, rs.at[u]).start()
            else:
                c = remote(src, dst, ss.at[d], rs.at[u], uly=to)
                c.start()
                sent.append(c)
    for s in range(nb):
        arrived(rq.at[s], s1q_r.at[s])
    pltpu.make_async_copy(rq.at[my_s, my_e], qo.at[u], s2q_r.at[u]).start()
    for d in znear:
        to = lax.rem(u + d, nz)
        c = remote(rq.at[to // kvh, lax.rem(to, kvh)], qo.at[u], s2q_s.at[d], s2q_r.at[u], uly=to)
        c.start()
        sent.append(c)

    row = lax.broadcasted_iota(jnp.int32, (tokens, tokens), 0)
    pos = row * tokens + lax.broadcasted_iota(jnp.int32, (tokens, tokens), 1) + my_s * stretch
    first = jnp.zeros((tokens, tokens), jnp.int32)
    start = jnp.int32(0)
    for n in range(lengths.shape[0]):
        first = jnp.where(pos >= start, start, first)
        start = start + lengths[n]
    lo_t[...] = jnp.transpose((first - (my_s - 1) * stretch - row * tokens).astype(jnp.float32))

    other = b + 1 - 2 * lax.rem(b, 2)
    half = nb // 2
    for cp, rs in ((1, s2c_r), (0, s2p_r)):
        for z in range(nz):
            arrived(kvo.at[:, cp * nz + z, b], rs.at[z])
        mine = kvo.at[:, cp * nz : (cp + 1) * nz, b]
        for d in range(1, half):
            c = remote(mine, mine, gy_s.at[cp * half + d], gy_r.at[cp * half + d], blk=lax.rem(b + 2 * d, nb))
            c.start()
            sent.append(c)
        c = remote(mine, mine, gc_s.at[cp * half], gc_r.at[cp * half], blk=other)
        c.start()
        sent.append(c)
    for cp in (1, 0):
        for d in range(1, half):
            block = kvo.at[:, cp * nz : (cp + 1) * nz, lax.rem(b + nb - 2 * d, nb)]
            arrived(block, gy_r.at[cp * half + d])
            c = remote(block, block, gc_s.at[cp * half + d], gc_r.at[cp * half + d], blk=other)
            c.start()
            sent.append(c)
    for cp in (1, 0):
        for d in range(half):
            arrived(kvo.at[:, cp * nz : (cp + 1) * nz, lax.rem(other + nb - 2 * d, nb)], gc_r.at[cp * half + d])

    scale = math.log2(math.e) / math.sqrt(DH)
    chunks = [(c, min(2, window - c)) for c in range(0, window, 2)]

    def one_tile(z, sc):
        qt = qo[z]
        lane = lax.broadcasted_iota(jnp.int32, (tokens, tokens), 1)
        lo = jnp.sum(jnp.where(lane == z, lo_t[...], 0.0), axis=1, keepdims=True).astype(jnp.int32)
        lo = jnp.broadcast_to(lo, (tokens, tokens))
        causal = lane <= lax.broadcasted_iota(jnp.int32, (tokens, tokens), 0)
        top = jnp.full((tokens, tokens), NEG, jnp.float32)
        for c, n in chunks:
            kt = kvo[0, pl.ds(z + c, n)].reshape(n * tokens, DH)
            s = lax.dot_general(qt, kt, (((1,), (1,)), ((), ())), preferred_element_type=jnp.float32)
            for j in range(n):
                seen = lane >= lo - (c + j) * tokens
                if c + j == window - 1:
                    seen = seen & causal
                sj = jnp.where(seen, s[:, j * tokens : (j + 1) * tokens], NEG)
                sc[:, (c + j) * tokens : (c + j + 1) * tokens] = sj
                top = jnp.maximum(top, sj)
        m = jnp.max(top, axis=1, keepdims=True)
        acc = jnp.zeros((tokens, 2 * DH), jnp.float32)
        for c, n in chunks:
            p = jnp.exp2((sc[:, c * tokens : (c + n) * tokens] - m) * scale).astype(jnp.bfloat16)
            vt = kvo[1, pl.ds(z + c, n)].reshape(n * tokens, DH)
            both = jnp.concatenate([vt, jnp.ones_like(vt)], axis=1)
            acc = acc + jnp.dot(p, both, preferred_element_type=jnp.float32)
        out = (acc[:, :DH] / acc[:, DH:]).astype(jnp.bfloat16)
        att[pl.ds(z * (tokens // att.shape[1]), tokens // att.shape[1])] = out.reshape(tokens // att.shape[1], att.shape[1], DH)

    def two_tiles(i, _):
        near_z = lax.rem(u + i + 1, nz)
        far_z = lax.rem(u + jnp.where(i == nz // 2 - 1, 0, nz - 1 - i), nz)
        for z in (near_z, far_z):
            arrived(qo.at[z], s2q_r.at[z])
        one_tile(near_z, sc.at[0])
        one_tile(far_z, sc.at[1])
        return 0

    lax.fori_loop(0, nz // 2, two_tiles, 0)

    for i in range(pieces):
        sa[i] = att[plan[my_s, i]]
    slot = my_e * nb + b
    for d, f in [(d, f) for f in range(kvh - 1, -1, -1) for d in near[::-1]] + [(0, f) for f in range(kvh - 1, -1, -1)]:
        tb, te = lax.rem(b + d, nb), lax.rem(my_e + f, kvh)
        src = sa.at[pl.ds((tb * kvh + te) * per, per)]
        if (d, f) == (0, 0):
            pltpu.make_async_copy(src, ra.at[slot], rt_r.at[slot]).start()
        else:
            c = remote(src, ra.at[slot], rt_s.at[d * kvh + f], rt_r.at[slot], blk=tb, uly=my_s * kvh + te)
            c.start()
            sent.append(c)
    for i in range(heads):
        arrived(ra.at[i], rt_r.at[i])
    for h in range(heads):
        o[:, h * DH : (h + 1) * DH] = ra[slot_of(hm, h, heads, kvh)].reshape(tokens, DH)
    for c in sent:
        c.wait_send()


def body(queries, keys, values, head_map, doc_lengths, plan):
    nb, nz = lax.axis_size("blk"), lax.axis_size("uly")
    tokens = queries.shape[0]
    kvh = keys.shape[1] // DH
    stretch = tokens * nz
    part = tokens // nb
    heads = head_map.shape[0]
    pieces = plan.shape[1]
    block = stretch // pieces
    bf = jnp.bfloat16
    dma = pltpu.SemaphoreType.DMA
    sm = pl.BlockSpec(memory_space=SMEM)
    hbm = pl.BlockSpec(memory_space=pl.ANY)
    return pl.pallas_call(
        functools.partial(fused_kernel, nb, nz),
        out_shape=jax.ShapeDtypeStruct((tokens, heads * DH), bf),
        in_specs=[sm, sm, sm, hbm, hbm, hbm],
        out_specs=pl.BlockSpec(memory_space=VMEM),
        scratch_shapes=[
            VMEM((tokens, heads * DH), bf),
            VMEM((nb, kvh, tokens, DH), bf),
            VMEM((nb, kvh, 2, part, DH), bf),
            VMEM((nb, kvh, tokens, DH), bf),
            VMEM((nb, kvh, 2, part, DH), bf),
            VMEM((nz, tokens, DH), bf),
            VMEM((2, 2 * nz, nb, part, DH), bf),
            VMEM((pieces, block, DH), bf),
            VMEM((pieces, block, DH), bf),
            VMEM((heads, tokens // block, block, DH), bf),
            VMEM((tokens, tokens), jnp.float32),
            VMEM((2, tokens, (nz + 1) * tokens), jnp.float32),
            [dma((n,)) for n in (nb, nb, nb, nb, nz, nz, nz, nz, nz, nz, nb, nb, nb, nb, heads, heads, 2 * kvh + 1)],
        ],
        compiler_params=pltpu.CompilerParams(collective_id=0, has_side_effects=True, vmem_limit_bytes=63 << 20),
        name="fused",
    )(head_map, doc_lengths, plan, queries, keys.reshape(nb, part, kvh * DH), values.reshape(nb, part, kvh * DH))


def solution(mesh):
    return jax.shard_map(
        body,
        mesh=mesh,
        in_specs=(
            P(("blk", "uly"), "tp"),
            P(("blk", "uly"), "tp"),
            P(("blk", "uly"), "tp"),
            P("tp"),
            P(),
            P(),
        ),
        out_specs=P(("blk", "uly"), "tp"),
        check_vma=False,
    )
```

```python
import functools
import math

import jax
import jax.numpy as jnp
from jax import lax
from jax.experimental import pallas as pl
from jax.experimental.pallas import tpu as pltpu
from jax.sharding import PartitionSpec as P

DH = 128
MESH = pl.DeviceIdType.MESH
VMEM = pltpu.VMEM
SMEM = pltpu.SMEM
NEG = -1e30


def slot_of(head_map, h, heads, kv_heads):
    per = heads // kv_heads
    mine = head_map[h]
    before = jnp.int32(0)
    for g in range(h):
        before += (head_map[g] == mine).astype(jnp.int32)
    return mine * per + before


def fused_kernel(nb, nz, hm_hbm, lengths_hbm, plan_hbm, q_hbm, k_hbm, v_hbm, o, q, sq, skv, rq, rkv, qo, kvo, att, sa, lo_t, sc, hm, lengths, plan, sems):
    b, u = lax.axis_index("blk"), lax.axis_index("uly")
    heads = hm.shape[0]
    tokens = q.shape[0]
    kvh = skv.shape[1]
    pieces = att.shape[0]
    per = pieces // (nb * kvh)
    stretch = tokens * nz
    window = nz + 1
    (s1q_s, s1q_r, s1k_s, s1k_r, s2q_s, s2q_r, s2c_s, s2c_r, s2p_s, s2p_r, gy_s, gy_r, gc_s, gc_r, rt_s, rt_r, in_s) = sems
    my_s, my_e = u // kvh, lax.rem(u, kvh)

    def remote(src, dst, ss, rs, **to):
        return pltpu.make_async_remote_copy(
            src_ref=src, dst_ref=dst, send_sem=ss, recv_sem=rs, device_id=to, device_id_type=MESH)

    def arrived(dst, sem):
        pltpu.make_async_copy(dst, dst, sem).wait()

    barrier = pltpu.get_barrier_semaphore()
    twin = [(d, f) for f in range(1, kvh) for d in range(1, nb)]
    for d in range(1, nb):
        pl.semaphore_signal(barrier, inc=1, device_id={"blk": lax.rem(b + d, nb)}, device_id_type=MESH)
    for d in range(1, nz):
        pl.semaphore_signal(barrier, inc=1, device_id={"uly": lax.rem(u + d, nz)}, device_id_type=MESH)
    for d, f in twin:
        pl.semaphore_signal(
            barrier, inc=1, device_id={"blk": lax.rem(b + d, nb), "uly": my_s * kvh + lax.rem(my_e + f, kvh)},
            device_id_type=MESH)
    loads = []
    for i, (ref, to) in enumerate(((hm_hbm, hm), (lengths_hbm, lengths), (plan_hbm, plan))):
        c = pltpu.make_async_copy(ref, to, in_s.at[2 * kvh + 1 + i])
        c.start()
        loads.append(c)
    for e in range(kvh):
        for i, ref in enumerate((k_hbm, v_hbm)):
            c = pltpu.make_async_copy(ref.at[:, :, e * DH : (e + 1) * DH], skv.at[:, e, i], in_s.at[2 * e + i])
            c.start()
            loads.append(c)
    load_q = pltpu.make_async_copy(q_hbm, q, in_s.at[2 * kvh])
    load_q.start()

    for c in loads:
        c.wait()
    slots = [slot_of(hm, h, heads, kvh) for h in range(heads)]

    def head_at(i):
        at = jnp.int32(0)
        for h in range(heads):
            at += h * (slots[h] == i).astype(jnp.int32)
        return at

    def pack(to):
        for e in range(kvh):
            sq[to, e] = q[:, pl.ds(head_at(e * nb + to) * DH, DH)]

    near = []
    for d in range(1, nb // 2 + 1):
        near += [d] if d == nb - d else [d, nb - d]
    load_q.wait()
    for d in [0] + near:
        pack(lax.rem(b + d, nb))
    pl.semaphore_wait(barrier, nb - 1 + nz - 1 + len(twin))

    sent = []
    for d in near:
        to = lax.rem(b + d, nb)
        c = remote(skv.at[to], rkv.at[b], s1k_s.at[d], s1k_r.at[b], blk=to)
        c.start()
        sent.append(c)
    pltpu.make_async_copy(skv.at[b], rkv.at[b], s1k_r.at[b]).start()
    for d in near:
        to = lax.rem(b + d, nb)
        c = remote(sq.at[to], rq.at[b], s1q_s.at[d], s1q_r.at[b], blk=to)
        c.start()
        sent.append(c)
    pltpu.make_async_copy(sq.at[b], rq.at[b], s1q_r.at[b]).start()
    for s in range(nb):
        arrived(rkv.at[s], s1k_r.at[s])

    znear = []
    for d in range(1, nz // 2 + 1):
        znear += [d] if d == nz - d else [d, nz - d]
    for cp, ss, rs in ((1, s2c_s, s2c_r), (0, s2p_s, s2p_r)):
        for d in znear[::-1] + [0]:
            to = lax.rem(u + d, nz)
            s, e = to // kvh, lax.rem(to, kvh)
            src = rkv.at[s if cp else lax.rem(s + nb - 1, nb), e]
            dst = kvo.at[:, cp * nz + u, b]
            if d == 0:
                pltpu.make_async_copy(src, dst, rs.at[u]).start()
            else:
                c = remote(src, dst, ss.at[d], rs.at[u], uly=to)
                c.start()
                sent.append(c)
    for s in range(nb):
        arrived(rq.at[s], s1q_r.at[s])
    pltpu.make_async_copy(rq.at[my_s, my_e], qo.at[u], s2q_r.at[u]).start()
    for d in znear[::-1]:
        to = lax.rem(u + d, nz)
        c = remote(rq.at[to // kvh, lax.rem(to, kvh)], qo.at[u], s2q_s.at[d], s2q_r.at[u], uly=to)
        c.start()
        sent.append(c)

    row = lax.broadcasted_iota(jnp.int32, (tokens, tokens), 0)
    pos = row * tokens + lax.broadcasted_iota(jnp.int32, (tokens, tokens), 1) + my_s * stretch
    first = jnp.zeros((tokens, tokens), jnp.int32)
    start = jnp.int32(0)
    for n in range(lengths.shape[0]):
        first = jnp.where(pos >= start, start, first)
        start = start + lengths[n]
    lo_t[...] = jnp.transpose((first - (my_s - 1) * stretch - row * tokens).astype(jnp.float32))

    other = b + 1 - 2 * lax.rem(b, 2)
    half = nb // 2
    for cp, rs in ((1, s2c_r), (0, s2p_r)):
        for z in range(nz):
            arrived(kvo.at[:, cp * nz + z, b], rs.at[z])
        mine = kvo.at[:, cp * nz : (cp + 1) * nz, b]
        for d in range(1, half):
            c = remote(mine, mine, gy_s.at[cp * half + d], gy_r.at[cp * half + d], blk=lax.rem(b + 2 * d, nb))
            c.start()
            sent.append(c)
        c = remote(mine, mine, gc_s.at[cp * half], gc_r.at[cp * half], blk=other)
        c.start()
        sent.append(c)
    for cp in (1, 0):
        for d in range(1, half):
            block = kvo.at[:, cp * nz : (cp + 1) * nz, lax.rem(b + nb - 2 * d, nb)]
            arrived(block, gy_r.at[cp * half + d])
            c = remote(block, block, gc_s.at[cp * half + d], gc_r.at[cp * half + d], blk=other)
            c.start()
            sent.append(c)
    for cp in (1, 0):
        for d in range(half):
            arrived(kvo.at[:, cp * nz : (cp + 1) * nz, lax.rem(other + nb - 2 * d, nb)], gc_r.at[cp * half + d])

    scale = math.log2(math.e) / math.sqrt(DH)
    chunks = [(c, min(2, window - c)) for c in range(0, window, 2)]

    def one_tile(z, sc):
        qt = qo[z]
        lane = lax.broadcasted_iota(jnp.int32, (tokens, tokens), 1)
        lo = jnp.sum(jnp.where(lane == z, lo_t[...], 0.0), axis=1, keepdims=True).astype(jnp.int32)
        lo = jnp.broadcast_to(lo, (tokens, tokens))
        causal = lane <= lax.broadcasted_iota(jnp.int32, (tokens, tokens), 0)
        top = jnp.full((tokens, tokens), NEG, jnp.float32)
        for c, n in chunks:
            kt = kvo[0, pl.ds(z + c, n)].reshape(n * tokens, DH)
            s = lax.dot_general(qt, kt, (((1,), (1,)), ((), ())), preferred_element_type=jnp.float32)
            for j in range(n):
                seen = lane >= lo - (c + j) * tokens
                if c + j == window - 1:
                    seen = seen & causal
                sj = jnp.where(seen, s[:, j * tokens : (j + 1) * tokens], NEG)
                sc[:, (c + j) * tokens : (c + j + 1) * tokens] = sj
                top = jnp.maximum(top, sj)
        m = jnp.max(top, axis=1, keepdims=True)
        acc = jnp.zeros((tokens, 2 * DH), jnp.float32)
        for c, n in chunks:
            p = jnp.exp2((sc[:, c * tokens : (c + n) * tokens] - m) * scale).astype(jnp.bfloat16)
            vt = kvo[1, pl.ds(z + c, n)].reshape(n * tokens, DH)
            both = jnp.concatenate([vt, jnp.ones_like(vt)], axis=1)
            acc = acc + jnp.dot(p, both, preferred_element_type=jnp.float32)
        out = (acc[:, :DH] / acc[:, DH:]).astype(jnp.bfloat16)
        att[pl.ds(z * (tokens // att.shape[1]), tokens // att.shape[1])] = out.reshape(tokens // att.shape[1], att.shape[1], DH)

    def two_tiles(i, _):
        near_z = lax.rem(u + nz // 2 - i, nz)
        far_z = lax.rem(u + jnp.where(i == 0, 0, nz // 2 + i), nz)
        for z in (near_z, far_z):
            arrived(qo.at[z], s2q_r.at[z])
        one_tile(near_z, sc.at[0])
        one_tile(far_z, sc.at[1])
        return 0

    lax.fori_loop(0, nz // 2, two_tiles, 0)

    for i in range(pieces):
        sa[i] = att[plan[my_s, i]]
    slot = my_e * nb + b
    for d, f in [(d, f) for f in range(kvh - 1, -1, -1) for d in near[::-1]] + [(0, f) for f in range(kvh - 1, -1, -1)]:
        tb, te = lax.rem(b + d, nb), lax.rem(my_e + f, kvh)
        src = sa.at[pl.ds((tb * kvh + te) * per, per)]
        if (d, f) == (0, 0):
            pltpu.make_async_copy(src, o.at[slot], rt_r.at[slot]).start()
        else:
            c = remote(src, o.at[slot], rt_s.at[d * kvh + f], rt_r.at[slot], blk=tb, uly=my_s * kvh + te)
            c.start()
            sent.append(c)
    for i in range(heads):
        arrived(o.at[i], rt_r.at[i])
    for c in sent:
        c.wait_send()


def place_kernel(kvh, hm, slots, o):
    heads = hm.shape[0]
    for h in range(heads):
        o[:, h * DH : (h + 1) * DH] = slots[slot_of(hm, h, heads, kvh)]


def body(queries, keys, values, head_map, doc_lengths, plan):
    nb, nz = lax.axis_size("blk"), lax.axis_size("uly")
    tokens = queries.shape[0]
    kvh = keys.shape[1] // DH
    stretch = tokens * nz
    part = tokens // nb
    heads = head_map.shape[0]
    pieces = plan.shape[1]
    block = stretch // pieces
    bf = jnp.bfloat16
    dma = pltpu.SemaphoreType.DMA
    sm = pl.BlockSpec(memory_space=SMEM)
    hbm = pl.BlockSpec(memory_space=pl.ANY)
    slots = pl.pallas_call(
        functools.partial(fused_kernel, nb, nz),
        out_shape=jax.ShapeDtypeStruct((heads, tokens // block, block, DH), bf),
        in_specs=[hbm] * 6,
        out_specs=hbm,
        scratch_shapes=[
            VMEM((tokens, heads * DH), bf),
            VMEM((nb, kvh, tokens, DH), bf),
            VMEM((nb, kvh, 2, part, DH), bf),
            VMEM((nb, kvh, tokens, DH), bf),
            VMEM((nb, kvh, 2, part, DH), bf),
            VMEM((nz, tokens, DH), bf),
            VMEM((2, 2 * nz, nb, part, DH), bf),
            VMEM((pieces, block, DH), bf),
            VMEM((pieces, block, DH), bf),
            VMEM((tokens, tokens), jnp.float32),
            VMEM((2, tokens, (nz + 1) * tokens), jnp.float32),
            SMEM(head_map.shape, jnp.int32),
            SMEM(doc_lengths.shape, jnp.int32),
            SMEM(plan.shape, jnp.int32),
            [dma((n,)) for n in (nb, nb, nb, nb, nz, nz, nz, nz, nz, nz, nb, nb, nb, nb, heads, heads, 2 * kvh + 4)],
        ],
        compiler_params=pltpu.CompilerParams(collective_id=0, has_side_effects=True, vmem_limit_bytes=63 << 20),
        name="fused",
    )(head_map, doc_lengths, plan, queries, keys.reshape(nb, part, kvh * DH), values.reshape(nb, part, kvh * DH))
    vm = pl.BlockSpec(memory_space=VMEM)
    return pl.pallas_call(
        functools.partial(place_kernel, kvh),
        out_shape=jax.ShapeDtypeStruct((tokens, heads * DH), bf),
        in_specs=[sm, vm],
        out_specs=vm,
        compiler_params=pltpu.CompilerParams(vmem_limit_bytes=63 << 20),
        name="place",
    )(head_map, slots.reshape(heads, tokens, DH))


def solution(mesh):
    return jax.shard_map(
        body,
        mesh=mesh,
        in_specs=(
            P(("blk", "uly"), "tp"),
            P(("blk", "uly"), "tp"),
            P(("blk", "uly"), "tp"),
            P("tp"),
            P(),
            P(),
        ),
        out_specs=P(("blk", "uly"), "tp"),
        check_vma=False,
    )
```

```python
import functools
import math

import jax
import jax.numpy as jnp
from jax import lax
from jax.experimental import pallas as pl
from jax.experimental.pallas import tpu as pltpu
from jax.sharding import PartitionSpec as P

DH = 128
MESH = pl.DeviceIdType.MESH
VMEM = pltpu.VMEM
SMEM = pltpu.SMEM
NEG = -1e30


def slot_of(head_map, h, heads, kv_heads):
    per = heads // kv_heads
    mine = head_map[h]
    before = jnp.int32(0)
    for g in range(h):
        before += (head_map[g] == mine).astype(jnp.int32)
    return mine * per + before


def fused_kernel(nb, nz, hm_hbm, lengths_hbm, plan_hbm, q_hbm, k_hbm, v_hbm, o, q, sq, skv, rq, rkv, qo, kvo, att, sa, lo_t, sc, hm, lengths, plan, sems):
    b, u = lax.axis_index("blk"), lax.axis_index("uly")
    heads = hm.shape[0]
    tokens = q.shape[0]
    kvh = skv.shape[1]
    pieces = att.shape[0]
    per = pieces // (nb * kvh)
    stretch = tokens * nz
    window = nz + 1
    (s1q_s, s1q_r, s1k_s, s1k_r, s2q_s, s2q_r, s2c_s, s2c_r, s2p_s, s2p_r, gy_s, gy_r, gc_s, gc_r, rt_s, rt_r, in_s) = sems
    my_s, my_e = u // kvh, lax.rem(u, kvh)

    def remote(src, dst, ss, rs, **to):
        return pltpu.make_async_remote_copy(
            src_ref=src, dst_ref=dst, send_sem=ss, recv_sem=rs, device_id=to, device_id_type=MESH)

    def arrived(dst, sem):
        pltpu.make_async_copy(dst, dst, sem).wait()

    barrier = pltpu.get_barrier_semaphore()
    twin = [(d, f) for f in range(1, kvh) for d in range(1, nb)]
    for d in sorted(range(1, nz), key=lambda d: -min(d, nz - d)):
        pl.semaphore_signal(barrier, inc=1, device_id={"uly": lax.rem(u + d, nz)}, device_id_type=MESH)
    for d in range(1, nb):
        pl.semaphore_signal(barrier, inc=1, device_id={"blk": lax.rem(b + d, nb)}, device_id_type=MESH)
    for d, f in twin:
        pl.semaphore_signal(
            barrier, inc=1, device_id={"blk": lax.rem(b + d, nb), "uly": my_s * kvh + lax.rem(my_e + f, kvh)},
            device_id_type=MESH)
    loads = []
    for i, (ref, to) in enumerate(((hm_hbm, hm), (lengths_hbm, lengths), (plan_hbm, plan))):
        c = pltpu.make_async_copy(ref, to, in_s.at[2 * kvh + 1 + i])
        c.start()
        loads.append(c)
    for e in range(kvh):
        for i, ref in enumerate((k_hbm, v_hbm)):
            c = pltpu.make_async_copy(ref.at[:, :, e * DH : (e + 1) * DH], skv.at[:, e, i], in_s.at[2 * e + i])
            c.start()
            loads.append(c)
    load_q = pltpu.make_async_copy(q_hbm, q, in_s.at[2 * kvh])
    load_q.start()

    for c in loads:
        c.wait()
    slots = [slot_of(hm, h, heads, kvh) for h in range(heads)]

    def head_at(i):
        at = jnp.int32(0)
        for h in range(heads):
            at += h * (slots[h] == i).astype(jnp.int32)
        return at

    def pack(to):
        for e in range(kvh):
            sq[to, e] = q[:, pl.ds(head_at(e * nb + to) * DH, DH)]

    near = []
    for d in range(1, nb // 2 + 1):
        near += [d] if d == nb - d else [d, nb - d]
    load_q.wait()
    for d in [0] + near:
        pack(lax.rem(b + d, nb))
    pl.semaphore_wait(barrier, nb - 1 + nz - 1 + len(twin))

    sent = []
    for d in near:
        to = lax.rem(b + d, nb)
        c = remote(skv.at[to], rkv.at[b], s1k_s.at[d], s1k_r.at[b], blk=to)
        c.start()
        sent.append(c)
    pltpu.make_async_copy(skv.at[b], rkv.at[b], s1k_r.at[b]).start()
    for d in near:
        to = lax.rem(b + d, nb)
        c = remote(sq.at[to], rq.at[b], s1q_s.at[d], s1q_r.at[b], blk=to)
        c.start()
        sent.append(c)
    pltpu.make_async_copy(sq.at[b], rq.at[b], s1q_r.at[b]).start()
    for s in range(nb):
        arrived(rkv.at[s], s1k_r.at[s])

    znear = []
    for d in range(1, nz // 2 + 1):
        znear += [d] if d == nz - d else [d, nz - d]
    for cp, ss, rs in ((1, s2c_s, s2c_r), (0, s2p_s, s2p_r)):
        for d in znear[::-1] + [0]:
            to = lax.rem(u + d, nz)
            s, e = to // kvh, lax.rem(to, kvh)
            src = rkv.at[s if cp else lax.rem(s + nb - 1, nb), e]
            dst = kvo.at[:, cp * nz + u, b]
            if d == 0:
                pltpu.make_async_copy(src, dst, rs.at[u]).start()
            else:
                c = remote(src, dst, ss.at[d], rs.at[u], uly=to)
                c.start()
                sent.append(c)
    for s in range(nb):
        arrived(rq.at[s], s1q_r.at[s])
    pltpu.make_async_copy(rq.at[my_s, my_e], qo.at[u], s2q_r.at[u]).start()
    for d in znear[::-1]:
        to = lax.rem(u + d, nz)
        c = remote(rq.at[to // kvh, lax.rem(to, kvh)], qo.at[u], s2q_s.at[d], s2q_r.at[u], uly=to)
        c.start()
        sent.append(c)

    row = lax.broadcasted_iota(jnp.int32, (tokens, tokens), 0)
    pos = row * tokens + lax.broadcasted_iota(jnp.int32, (tokens, tokens), 1) + my_s * stretch
    first = jnp.zeros((tokens, tokens), jnp.int32)
    start = jnp.int32(0)
    for n in range(lengths.shape[0]):
        first = jnp.where(pos >= start, start, first)
        start = start + lengths[n]
    lo_t[...] = jnp.transpose((first - (my_s - 1) * stretch - row * tokens).astype(jnp.float32))

    other = b + 1 - 2 * lax.rem(b, 2)
    half = nb // 2
    for cp, rs in ((1, s2c_r), (0, s2p_r)):
        for z in range(nz):
            arrived(kvo.at[:, cp * nz + z, b], rs.at[z])
        mine = kvo.at[:, cp * nz : (cp + 1) * nz, b]
        for d in range(1, half):
            c = remote(mine, mine, gy_s.at[cp * half + d], gy_r.at[cp * half + d], blk=lax.rem(b + 2 * d, nb))
            c.start()
            sent.append(c)
        c = remote(mine, mine, gc_s.at[cp * half], gc_r.at[cp * half], blk=other)
        c.start()
        sent.append(c)
    for cp in (1, 0):
        for d in range(1, half):
            block = kvo.at[:, cp * nz : (cp + 1) * nz, lax.rem(b + nb - 2 * d, nb)]
            arrived(block, gy_r.at[cp * half + d])
            c = remote(block, block, gc_s.at[cp * half + d], gc_r.at[cp * half + d], blk=other)
            c.start()
            sent.append(c)
    for cp in (1, 0):
        for d in range(half):
            arrived(kvo.at[:, cp * nz : (cp + 1) * nz, lax.rem(other + nb - 2 * d, nb)], gc_r.at[cp * half + d])

    scale = math.log2(math.e) / math.sqrt(DH)
    chunks = [(c, min(2, window - c)) for c in range(0, window, 2)]

    def one_tile(z, sc):
        qt = qo[z]
        lane = lax.broadcasted_iota(jnp.int32, (tokens, tokens), 1)
        lo = jnp.sum(jnp.where(lane == z, lo_t[...], 0.0), axis=1, keepdims=True).astype(jnp.int32)
        lo = jnp.broadcast_to(lo, (tokens, tokens))
        causal = lane <= lax.broadcasted_iota(jnp.int32, (tokens, tokens), 0)
        top = jnp.full((tokens, tokens), NEG, jnp.float32)
        for c, n in chunks:
            kt = kvo[0, pl.ds(z + c, n)].reshape(n * tokens, DH)
            s = lax.dot_general(qt, kt, (((1,), (1,)), ((), ())), preferred_element_type=jnp.float32)
            for j in range(n):
                seen = lane >= lo - (c + j) * tokens
                if c + j == window - 1:
                    seen = seen & causal
                sj = jnp.where(seen, s[:, j * tokens : (j + 1) * tokens], NEG)
                sc[:, (c + j) * tokens : (c + j + 1) * tokens] = sj
                top = jnp.maximum(top, sj)
        m = jnp.max(top, axis=1, keepdims=True)
        acc = jnp.zeros((tokens, 2 * DH), jnp.float32)
        for c, n in chunks:
            p = jnp.exp2((sc[:, c * tokens : (c + n) * tokens] - m) * scale).astype(jnp.bfloat16)
            vt = kvo[1, pl.ds(z + c, n)].reshape(n * tokens, DH)
            both = jnp.concatenate([vt, jnp.ones_like(vt)], axis=1)
            acc = acc + jnp.dot(p, both, preferred_element_type=jnp.float32)
        out = (acc[:, :DH] / acc[:, DH:]).astype(jnp.bfloat16)
        att[pl.ds(z * (tokens // att.shape[1]), tokens // att.shape[1])] = out.reshape(tokens // att.shape[1], att.shape[1], DH)

    def two_tiles(i, _):
        near_z = lax.rem(u + nz // 2 - i, nz)
        far_z = lax.rem(u + jnp.where(i == 0, 0, nz // 2 + i), nz)
        for z in (near_z, far_z):
            arrived(qo.at[z], s2q_r.at[z])
        one_tile(near_z, sc.at[0])
        one_tile(far_z, sc.at[1])
        return 0

    lax.fori_loop(0, nz // 2, two_tiles, 0)

    slot = my_e * nb + b
    for d, f in [(d, f) for f in range(kvh - 1, -1, -1) for d in near[::-1]] + [(0, f) for f in range(kvh - 1, -1, -1)]:
        tb, te = lax.rem(b + d, nb), lax.rem(my_e + f, kvh)
        at = (tb * kvh + te) * per
        for i in range(per):
            sa[at + i] = att[plan[my_s, at + i]]
        src = sa.at[pl.ds(at, per)]
        if (d, f) == (0, 0):
            pltpu.make_async_copy(src, o.at[slot], rt_r.at[slot]).start()
        else:
            c = remote(src, o.at[slot], rt_s.at[d * kvh + f], rt_r.at[slot], blk=tb, uly=my_s * kvh + te)
            c.start()
            sent.append(c)
    for i in range(heads):
        arrived(o.at[i], rt_r.at[i])
    for c in sent:
        c.wait_send()


def place_kernel(kvh, parts, hm_hbm, slots, o, hm, x, y, in_s, out_s, hm_s):
    heads, tokens = x.shape[0], x.shape[1]
    rows = tokens // parts
    get_hm = pltpu.make_async_copy(hm_hbm, hm, hm_s.at[0])
    get_hm.start()
    gets, puts = [], []
    for t in range(parts):
        at = slice(t * rows, (t + 1) * rows)
        gets.append(pltpu.make_async_copy(slots.at[:, at], x.at[:, at], in_s.at[t]))
        puts.append(pltpu.make_async_copy(y.at[at], o.at[at], out_s.at[t]))
        gets[t].start()
    get_hm.wait()
    source = [slot_of(hm, h, heads, kvh) for h in range(heads)]
    for t in range(parts):
        at = slice(t * rows, (t + 1) * rows)
        gets[t].wait()
        for h in range(heads):
            y[at, h * DH : (h + 1) * DH] = x[source[h], at]
        puts[t].start()
    for c in puts:
        c.wait()


def body(queries, keys, values, head_map, doc_lengths, plan):
    nb, nz = lax.axis_size("blk"), lax.axis_size("uly")
    tokens = queries.shape[0]
    kvh = keys.shape[1] // DH
    stretch = tokens * nz
    part = tokens // nb
    heads = head_map.shape[0]
    pieces = plan.shape[1]
    block = stretch // pieces
    bf = jnp.bfloat16
    dma = pltpu.SemaphoreType.DMA
    hbm = pl.BlockSpec(memory_space=pl.ANY)
    slots = pl.pallas_call(
        functools.partial(fused_kernel, nb, nz),
        out_shape=jax.ShapeDtypeStruct((heads, tokens // block, block, DH), bf),
        in_specs=[hbm] * 6,
        out_specs=hbm,
        scratch_shapes=[
            VMEM((tokens, heads * DH), bf),
            VMEM((nb, kvh, tokens, DH), bf),
            VMEM((nb, kvh, 2, part, DH), bf),
            VMEM((nb, kvh, tokens, DH), bf),
            VMEM((nb, kvh, 2, part, DH), bf),
            VMEM((nz, tokens, DH), bf),
            VMEM((2, 2 * nz, nb, part, DH), bf),
            VMEM((pieces, block, DH), bf),
            VMEM((pieces, block, DH), bf),
            VMEM((tokens, tokens), jnp.float32),
            VMEM((2, tokens, (nz + 1) * tokens), jnp.float32),
            SMEM(head_map.shape, jnp.int32),
            SMEM(doc_lengths.shape, jnp.int32),
            SMEM(plan.shape, jnp.int32),
            [dma((n,)) for n in (nb, nb, nb, nb, nz, nz, nz, nz, nz, nz, nb, nb, nb, nb, heads, heads, 2 * kvh + 4)],
        ],
        compiler_params=pltpu.CompilerParams(collective_id=0, has_side_effects=True, vmem_limit_bytes=63 << 20),
        name="fused",
    )(head_map, doc_lengths, plan, queries, keys.reshape(nb, part, kvh * DH), values.reshape(nb, part, kvh * DH))
    parts = 4
    return pl.pallas_call(
        functools.partial(place_kernel, kvh, parts),
        out_shape=jax.ShapeDtypeStruct((tokens, heads * DH), bf),
        in_specs=[hbm, hbm],
        out_specs=hbm,
        scratch_shapes=[
            SMEM(head_map.shape, jnp.int32),
            VMEM((heads, tokens, DH), bf),
            VMEM((tokens, heads * DH), bf),
            dma((parts,)),
            dma((parts,)),
            dma((1,)),
        ],
        compiler_params=pltpu.CompilerParams(vmem_limit_bytes=63 << 20),
        name="place",
    )(head_map, slots.reshape(heads, tokens, DH))


def solution(mesh):
    return jax.shard_map(
        body,
        mesh=mesh,
        in_specs=(
            P(("blk", "uly"), "tp"),
            P(("blk", "uly"), "tp"),
            P(("blk", "uly"), "tp"),
            P("tp"),
            P(),
            P(),
        ),
        out_specs=P(("blk", "uly"), "tp"),
        check_vma=False,
    )
```

```python
import functools
import math

import jax
import jax.numpy as jnp
from jax import lax
from jax.experimental import pallas as pl
from jax.experimental.pallas import tpu as pltpu
from jax.sharding import PartitionSpec as P

DH = 128
MESH = pl.DeviceIdType.MESH
VMEM = pltpu.VMEM
SMEM = pltpu.SMEM
NEG = -1e30


def slot_of(head_map, h, heads, kv_heads):
    per = heads // kv_heads
    mine = head_map[h]
    before = jnp.int32(0)
    for g in range(h):
        before += (head_map[g] == mine).astype(jnp.int32)
    return mine * per + before


def fused_kernel(nb, nz, hm_hbm, lengths_hbm, plan_hbm, q_hbm, k_hbm, v_hbm, o, q, sq, skv, rq, rkv, qo, kvo, att, sa, lo_t, sc, hm, lengths, plan, sems):
    b, u = lax.axis_index("blk"), lax.axis_index("uly")
    heads = hm.shape[0]
    tokens = q.shape[0]
    kvh = skv.shape[1]
    pieces = att.shape[0]
    per = pieces // (nb * kvh)
    stretch = tokens * nz
    window = nz + 1
    (s1q_s, s1q_r, s1k_s, s1k_r, s2q_s, s2q_r, s2c_s, s2c_r, s2p_s, s2p_r, gy_s, gy_r, gc_s, gc_r, rt_s, rt_r, in_s) = sems
    my_s, my_e = u // kvh, lax.rem(u, kvh)

    def remote(src, dst, ss, rs, **to):
        return pltpu.make_async_remote_copy(
            src_ref=src, dst_ref=dst, send_sem=ss, recv_sem=rs, device_id=to, device_id_type=MESH)

    def arrived(dst, sem):
        pltpu.make_async_copy(dst, dst, sem).wait()

    barrier = pltpu.get_barrier_semaphore()
    twin = [(d, f) for f in range(1, kvh) for d in range(1, nb)]
    for d in sorted(range(1, nz), key=lambda d: -min(d, nz - d)):
        pl.semaphore_signal(barrier, inc=1, device_id={"uly": lax.rem(u + d, nz)}, device_id_type=MESH)
    for d in range(1, nb):
        pl.semaphore_signal(barrier, inc=1, device_id={"blk": lax.rem(b + d, nb)}, device_id_type=MESH)
    for d, f in twin:
        pl.semaphore_signal(
            barrier, inc=1, device_id={"blk": lax.rem(b + d, nb), "uly": my_s * kvh + lax.rem(my_e + f, kvh)},
            device_id_type=MESH)
    loads = []
    for i, (ref, to) in enumerate(((hm_hbm, hm), (lengths_hbm, lengths), (plan_hbm, plan))):
        c = pltpu.make_async_copy(ref, to, in_s.at[2 * kvh + 1 + i])
        c.start()
        loads.append(c)
    for e in range(kvh):
        for i, ref in enumerate((k_hbm, v_hbm)):
            c = pltpu.make_async_copy(ref.at[:, :, e * DH : (e + 1) * DH], skv.at[:, e, i], in_s.at[2 * e + i])
            c.start()
            loads.append(c)
    load_q = pltpu.make_async_copy(q_hbm, q, in_s.at[2 * kvh])
    load_q.start()

    for c in loads:
        c.wait()
    slots = [slot_of(hm, h, heads, kvh) for h in range(heads)]

    def head_at(i):
        at = jnp.int32(0)
        for h in range(heads):
            at += h * (slots[h] == i).astype(jnp.int32)
        return at

    def pack(to):
        for e in range(kvh):
            sq[to, e] = q[:, pl.ds(head_at(e * nb + to) * DH, DH)]

    near = []
    for d in range(1, nb // 2 + 1):
        near += [d] if d == nb - d else [d, nb - d]
    load_q.wait()
    for d in [0] + near:
        pack(lax.rem(b + d, nb))
    pl.semaphore_wait(barrier, nb - 1 + nz - 1 + len(twin))

    sent = []
    for d in near:
        to = lax.rem(b + d, nb)
        c = remote(skv.at[to], rkv.at[b], s1k_s.at[d], s1k_r.at[b], blk=to)
        c.start()
        sent.append(c)
    pltpu.make_async_copy(skv.at[b], rkv.at[b], s1k_r.at[b]).start()
    for d in near:
        to = lax.rem(b + d, nb)
        c = remote(sq.at[to], rq.at[b], s1q_s.at[d], s1q_r.at[b], blk=to)
        c.start()
        sent.append(c)
    pltpu.make_async_copy(sq.at[b], rq.at[b], s1q_r.at[b]).start()
    for s in range(nb):
        arrived(rkv.at[s], s1k_r.at[s])

    znear = []
    for d in range(1, nz // 2 + 1):
        znear += [d] if d == nz - d else [d, nz - d]
    for cp, ss, rs in ((1, s2c_s, s2c_r), (0, s2p_s, s2p_r)):
        for d in znear[::-1] + [0]:
            to = lax.rem(u + d, nz)
            s, e = to // kvh, lax.rem(to, kvh)
            src = rkv.at[s if cp else lax.rem(s + nb - 1, nb), e]
            dst = kvo.at[:, cp * nz + u, b]
            if d == 0:
                pltpu.make_async_copy(src, dst, rs.at[u]).start()
            else:
                c = remote(src, dst, ss.at[d], rs.at[u], uly=to)
                c.start()
                sent.append(c)
    for s in range(nb):
        arrived(rq.at[s], s1q_r.at[s])
    pltpu.make_async_copy(rq.at[my_s, my_e], qo.at[u], s2q_r.at[u]).start()
    for d in znear[::-1]:
        to = lax.rem(u + d, nz)
        c = remote(rq.at[to // kvh, lax.rem(to, kvh)], qo.at[u], s2q_s.at[d], s2q_r.at[u], uly=to)
        c.start()
        sent.append(c)

    row = lax.broadcasted_iota(jnp.int32, (tokens, tokens), 0)
    pos = row * tokens + lax.broadcasted_iota(jnp.int32, (tokens, tokens), 1) + my_s * stretch
    first = jnp.zeros((tokens, tokens), jnp.int32)
    start = jnp.int32(0)
    for n in range(lengths.shape[0]):
        first = jnp.where(pos >= start, start, first)
        start = start + lengths[n]
    lo_t[...] = jnp.transpose((first - (my_s - 1) * stretch - row * tokens).astype(jnp.float32))

    other = b + 1 - 2 * lax.rem(b, 2)
    half = nb // 2
    for cp, rs in ((1, s2c_r), (0, s2p_r)):
        for z in range(nz):
            arrived(kvo.at[:, cp * nz + z, b], rs.at[z])
        mine = kvo.at[:, cp * nz : (cp + 1) * nz, b]
        for d in sorted(range(1, half), key=lambda d: -min(d, half - d)):
            c = remote(mine, mine, gy_s.at[cp * half + d], gy_r.at[cp * half + d], blk=lax.rem(b + 2 * d, nb))
            c.start()
            sent.append(c)
        c = remote(mine, mine, gc_s.at[cp * half], gc_r.at[cp * half], blk=other)
        c.start()
        sent.append(c)
    for cp in (1, 0):
        for d in sorted(range(1, half), key=lambda d: min(d, half - d)):
            block = kvo.at[:, cp * nz : (cp + 1) * nz, lax.rem(b + nb - 2 * d, nb)]
            arrived(block, gy_r.at[cp * half + d])
            c = remote(block, block, gc_s.at[cp * half + d], gc_r.at[cp * half + d], blk=other)
            c.start()
            sent.append(c)
    for cp in (1, 0):
        for d in range(half):
            arrived(kvo.at[:, cp * nz : (cp + 1) * nz, lax.rem(other + nb - 2 * d, nb)], gc_r.at[cp * half + d])

    scale = math.log2(math.e) / math.sqrt(DH)
    chunks = [(c, min(2, window - c)) for c in range(0, window, 2)]

    def one_tile(z, sc):
        qt = qo[z]
        lane = lax.broadcasted_iota(jnp.int32, (tokens, tokens), 1)
        lo = jnp.sum(jnp.where(lane == z, lo_t[...], 0.0), axis=1, keepdims=True).astype(jnp.int32)
        lo = jnp.broadcast_to(lo, (tokens, tokens))
        causal = lane <= lax.broadcasted_iota(jnp.int32, (tokens, tokens), 0)
        top = jnp.full((tokens, tokens), NEG, jnp.float32)
        for c, n in chunks:
            kt = kvo[0, pl.ds(z + c, n)].reshape(n * tokens, DH)
            s = lax.dot_general(qt, kt, (((1,), (1,)), ((), ())), preferred_element_type=jnp.float32)
            for j in range(n):
                seen = lane >= lo - (c + j) * tokens
                if c + j == window - 1:
                    seen = seen & causal
                sj = jnp.where(seen, s[:, j * tokens : (j + 1) * tokens], NEG)
                sc[:, (c + j) * tokens : (c + j + 1) * tokens] = sj
                top = jnp.maximum(top, sj)
        m = jnp.max(top, axis=1, keepdims=True)
        acc = jnp.zeros((tokens, 2 * DH), jnp.float32)
        for c, n in chunks:
            p = jnp.exp2((sc[:, c * tokens : (c + n) * tokens] - m) * scale).astype(jnp.bfloat16)
            vt = kvo[1, pl.ds(z + c, n)].reshape(n * tokens, DH)
            both = jnp.concatenate([vt, jnp.ones_like(vt)], axis=1)
            acc = acc + jnp.dot(p, both, preferred_element_type=jnp.float32)
        out = (acc[:, :DH] / acc[:, DH:]).astype(jnp.bfloat16)
        att[pl.ds(z * (tokens // att.shape[1]), tokens // att.shape[1])] = out.reshape(tokens // att.shape[1], att.shape[1], DH)

    def two_tiles(i, _):
        near_z = lax.rem(u + nz // 2 - i, nz)
        far_z = lax.rem(u + jnp.where(i == 0, 0, nz // 2 + i), nz)
        for z in (near_z, far_z):
            arrived(qo.at[z], s2q_r.at[z])
        one_tile(near_z, sc.at[0])
        one_tile(far_z, sc.at[1])
        return 0

    lax.fori_loop(0, nz // 2, two_tiles, 0)

    slot = my_e * nb + b
    for d, f in [(d, f) for f in range(kvh - 1, -1, -1) for d in near[::-1]] + [(0, f) for f in range(kvh - 1, -1, -1)]:
        tb, te = lax.rem(b + d, nb), lax.rem(my_e + f, kvh)
        at = (tb * kvh + te) * per
        for i in range(per):
            sa[at + i] = att[plan[my_s, at + i]]
        src = sa.at[pl.ds(at, per)]
        if (d, f) == (0, 0):
            pltpu.make_async_copy(src, o.at[slot], rt_r.at[slot]).start()
        else:
            c = remote(src, o.at[slot], rt_s.at[d * kvh + f], rt_r.at[slot], blk=tb, uly=my_s * kvh + te)
            c.start()
            sent.append(c)
    for i in range(heads):
        arrived(o.at[i], rt_r.at[i])
    for c in sent:
        c.wait_send()


def place_kernel(kvh, parts, hm_hbm, slots, o, hm, x, y, in_s, out_s, hm_s):
    heads, tokens = x.shape[0], x.shape[1]
    rows = tokens // parts
    get_hm = pltpu.make_async_copy(hm_hbm, hm, hm_s.at[0])
    get_hm.start()
    gets, puts = [], []
    for t in range(parts):
        at = slice(t * rows, (t + 1) * rows)
        gets.append(pltpu.make_async_copy(slots.at[:, at], x.at[:, at], in_s.at[t]))
        puts.append(pltpu.make_async_copy(y.at[at], o.at[at], out_s.at[t]))
        gets[t].start()
    get_hm.wait()
    source = [slot_of(hm, h, heads, kvh) for h in range(heads)]
    for t in range(parts):
        at = slice(t * rows, (t + 1) * rows)
        gets[t].wait()
        for h in range(heads):
            y[at, h * DH : (h + 1) * DH] = x[source[h], at]
        puts[t].start()
    for c in puts:
        c.wait()


def body(queries, keys, values, head_map, doc_lengths, plan):
    nb, nz = lax.axis_size("blk"), lax.axis_size("uly")
    tokens = queries.shape[0]
    kvh = keys.shape[1] // DH
    stretch = tokens * nz
    part = tokens // nb
    heads = head_map.shape[0]
    pieces = plan.shape[1]
    block = stretch // pieces
    bf = jnp.bfloat16
    dma = pltpu.SemaphoreType.DMA
    hbm = pl.BlockSpec(memory_space=pl.ANY)
    slots = pl.pallas_call(
        functools.partial(fused_kernel, nb, nz),
        out_shape=jax.ShapeDtypeStruct((heads, tokens // block, block, DH), bf),
        in_specs=[hbm] * 6,
        out_specs=hbm,
        scratch_shapes=[
            VMEM((tokens, heads * DH), bf),
            VMEM((nb, kvh, tokens, DH), bf),
            VMEM((nb, kvh, 2, part, DH), bf),
            VMEM((nb, kvh, tokens, DH), bf),
            VMEM((nb, kvh, 2, part, DH), bf),
            VMEM((nz, tokens, DH), bf),
            VMEM((2, 2 * nz, nb, part, DH), bf),
            VMEM((pieces, block, DH), bf),
            VMEM((pieces, block, DH), bf),
            VMEM((tokens, tokens), jnp.float32),
            VMEM((2, tokens, (nz + 1) * tokens), jnp.float32),
            SMEM(head_map.shape, jnp.int32),
            SMEM(doc_lengths.shape, jnp.int32),
            SMEM(plan.shape, jnp.int32),
            [dma((n,)) for n in (nb, nb, nb, nb, nz, nz, nz, nz, nz, nz, nb, nb, nb, nb, heads, heads, 2 * kvh + 4)],
        ],
        compiler_params=pltpu.CompilerParams(collective_id=0, has_side_effects=True, vmem_limit_bytes=63 << 20),
        name="fused",
    )(head_map, doc_lengths, plan, queries, keys.reshape(nb, part, kvh * DH), values.reshape(nb, part, kvh * DH))
    parts = 4
    return pl.pallas_call(
        functools.partial(place_kernel, kvh, parts),
        out_shape=jax.ShapeDtypeStruct((tokens, heads * DH), bf),
        in_specs=[hbm, hbm],
        out_specs=hbm,
        scratch_shapes=[
            SMEM(head_map.shape, jnp.int32),
            VMEM((heads, tokens, DH), bf),
            VMEM((tokens, heads * DH), bf),
            dma((parts,)),
            dma((parts,)),
            dma((1,)),
        ],
        compiler_params=pltpu.CompilerParams(vmem_limit_bytes=63 << 20),
        name="place",
    )(head_map, slots.reshape(heads, tokens, DH))


def solution(mesh):
    return jax.shard_map(
        body,
        mesh=mesh,
        in_specs=(
            P(("blk", "uly"), "tp"),
            P(("blk", "uly"), "tp"),
            P(("blk", "uly"), "tp"),
            P("tp"),
            P(),
            P(),
        ),
        out_specs=P(("blk", "uly"), "tp"),
        check_vma=False,
    )
```
